512 devices in a mesh: grp: 2 (over y_hi), row: 32 (over z, core), col: 8 (over x, y_lo).
Axes of the slice: x: 4, y: 4 (y_hi: 2, y_lo: 2; y = y_hi * 2 + y_lo), z: 16, core: 2. Of those that a mesh axis runs over, the one named last changes fastest.
Arguments:
- queries: bfloat16 [32, 8, 8192], P('row', None, 'col'), may hold values from -160 to 160
- tree_kv: bfloat16 [32, 8, 2, 1024], P('row', None, None, 'col'), may hold values from -6 to 6
- cache: bfloat16 [32, 2, 4096, 1024], P('row', None, 'grp', 'col'), may hold values from -6 to 6
- ctx_len: int32 [32], P('row'), may hold values from 512 to 4096, as said below
- parents: int32 [32, 8], P('row'), may hold values from -1 to 6, as said below
- stream: bfloat16 [256, 8192], P('row', ('grp', 'col')), may hold values from -64 to 64
- out_weight: bfloat16 [8192, 8192], P('row', ('grp', 'col')), may hold values from -0.0625 to 0.0625
- norm_gain: float32 [8192], P(('grp', 'col')), may hold values from 0.1 to 1.9
- gate_weight: bfloat16 [8192, 28672], P(('grp', 'col'), 'row'), may hold values from -0.0625 to 0.0625
- up_weight: bfloat16 [8192, 28672], P(('grp', 'col'), 'row'), may hold values from -0.0625 to 0.0625
- down_weight: bfloat16 [28672, 8192], P('row', ('grp', 'col')), may hold values from -0.03125 to 0.03125
Outputs:
- attended: bfloat16 [256, 8192], P('row', ('grp', 'col'))
- layer_output: bfloat16 [256, 8192], P('row', ('grp', 'col'))
The draws below stay inside these ranges and needn't reach their ends.
Inputs may be any that keep to these rules, and one draw needn't show every extreme that they name: Request r's context occupies its first ctx_len[r] cache positions; some request fills all 4096. `parents`: node 0 of each tree is its root, marked -1; node i > 0 has a parent below i.
All inputs are finite; a program needn't handle non-finite values.
Results may differ from the reference program's by a relative error of at most 0.015.
Values may be sent and summed in bfloat16 or wider, within the bound.
No kernel may reach another device: no remote copies, remote signals or barrier semaphores. Data moves between devices by JAX's collectives and lax.ppermute only.
A program may use at most 64 MiB of HBM per device.

```python
import math
import jax
import jax.numpy as jnp
from jax import lax

D = 8192
FF = 28672
HQ = 64
KVH = 8
HD = 128
NODES = 8
REQS = 32
CTX = 4096
TOKENS = 256
N_GRP = 2
N_ROW = 32
N_COL = 8


def shared_keys(key):
    sample = jax.random.normal(key, (REQS, CTX, KVH * HD), jnp.float32)
    sample = sample.at[:, 1, :].set(sample[:, 1, :])
    return jnp.clip(sample, -6.0, 6.0)


def draw_cache(key, part):
    cached_keys = shared_keys(key)
    key = jax.random.fold_in(key, 5)
    cached_values = jnp.clip(jax.random.normal(key, (REQS, CTX, KVH * HD), jnp.float32), -6.0, 6.0)
    return jnp.stack([cached_keys, cached_values], axis=1).astype(jnp.bfloat16)


def draw_queries(key, part):
    key = jax.random.fold_in(key, 7)
    sample = jax.random.normal(key, (REQS, NODES, HQ * HD), jnp.float32) * 2.5
    return jnp.clip(sample, -16.0, 16.0).astype(jnp.bfloat16)


def draw_ctx_len(key, part):
    key = jax.random.fold_in(key, 3)
    first_key, second_key = jax.random.split(key)
    lengths = jax.random.randint(first_key, (REQS,), CTX // 8, CTX + 1, dtype=jnp.int32)
    chosen = jax.random.randint(second_key, (), 0, REQS, dtype=jnp.int32)
    return jnp.where(jnp.arange(REQS, dtype=jnp.int32) == chosen, CTX, lengths).astype(jnp.int32)


def draw_parents(key, part):
    key = jax.random.fold_in(key, 9)
    first_key, second_key = jax.random.split(key)
    node_ids = jnp.arange(NODES, dtype=jnp.int32)
    upper = jnp.maximum(node_ids, 1)
    picked = jax.random.randint(first_key, (REQS, NODES), 0, upper[None, :], dtype=jnp.int32)
    chosen = jax.random.randint(second_key, (), 0, REQS, dtype=jnp.int32)
    request_ids = jnp.arange(REQS, dtype=jnp.int32)
    forced = (request_ids[:, None] == chosen) & (node_ids[None, :] == NODES - 1)
    picked = jnp.where(forced, NODES - 2, picked)
    return jnp.where(node_ids[None, :] == 0, -1, picked).astype(jnp.int32)


def draw_stream(key, part):
    key = jax.random.fold_in(key, 11)
    keys_split = jax.random.split(key, 3)
    rising = 0.6 + 1.2 * jnp.arange(D, dtype=jnp.float32) / D
    column = jnp.exp(jax.random.uniform(keys_split[0], (1, D), jnp.float32, -1.15, 1.15)) * rising[None, :]
    row_scale = jnp.exp(jax.random.uniform(keys_split[1], (TOKENS, 1), jnp.float32, -0.7, 0.7))
    sample = jnp.clip(jax.random.normal(keys_split[2], (TOKENS, D), jnp.float32), -5.0, 5.0)
    return jnp.clip(sample * column * row_scale, -64.0, 64.0).astype(jnp.bfloat16)


def block_scale(rng, dims, cuts, low, largest):
    def one(dim, blocks):
        steps = jax.random.uniform(jax.random.fold_in(jax.random.fold_in(rng, 6), dim), (blocks,), jnp.float32, low / len(cuts), largest / len(cuts))
        return jnp.repeat(jnp.exp(steps), dims[dim] // blocks).reshape((-1,) + (1,) * (len(dims) - dim - 1))

    loudness = one(*cuts[0])
    for cut in cuts[1:]:
        loudness = loudness * one(*cut)
    return loudness


def scatter_about(stream_key, extent, spread, limit, cuts=(), held_as=jnp.bfloat16):
    values = jax.random.normal(stream_key, extent, jnp.float32) * spread
    if len(cuts) > 0:
        values = block_scale(stream_key, extent, cuts, -0.22, 0.18) * values
    return jnp.clip(values, min=-limit, max=limit).astype(held_as)


def setup_inputs(seed: int = 0) -> dict:
    arg_keys = jax.random.split(jax.random.key(seed), 12)
    queries = draw_queries(jax.random.fold_in(arg_keys[11], 71), 0)
    tree_kv = scatter_about(arg_keys[1], (REQS, NODES, 2, KVH * HD), 1.0, 6.0, ((0, 32), (3, 8)))
    cache = draw_cache(jax.random.fold_in(arg_keys[11], 71), 0)
    ctx_len = draw_ctx_len(jax.random.fold_in(arg_keys[11], 71), 0)
    parents = draw_parents(jax.random.fold_in(arg_keys[11], 71), 0)
    stream = draw_stream(jax.random.fold_in(arg_keys[11], 71), 0)
    out_weight = scatter_about(arg_keys[6], (HQ * HD, D), (HQ * HD) ** -0.5, 0.0625, ((0, 32), (1, 16)))
    norm_gain = jnp.clip(1.0 + 0.18 * jax.random.normal(arg_keys[7], (D,), jnp.float32), 0.1, 1.9)
    gate_weight = scatter_about(arg_keys[8], (D, FF), D ** -0.5, 0.0625, ((0, 16), (1, 32)))
    up_weight = scatter_about(arg_keys[9], (D, FF), D ** -0.5, 0.0625, ((0, 16), (1, 32)))
    down_weight = scatter_about(arg_keys[10], (FF, D), FF ** -0.5, 0.03125, ((0, 32), (1, 16)))
    return {"queries": queries, "tree_kv": tree_kv, "cache": cache, "ctx_len": ctx_len, "parents": parents, "stream": stream, "out_weight": out_weight, "norm_gain": norm_gain, "gate_weight": gate_weight, "up_weight": up_weight, "down_weight": down_weight}


FLOOR = -1e+30
EPSILON = 1e-05
HIGHEST = lax.Precision.HIGHEST

def reach_table(parent_row):
    node_ids = jnp.arange(NODES, dtype=jnp.int32)
    parent_hot = (parent_row[:, None] == node_ids[None, :]).astype(jnp.float32)
    identity = jnp.eye(NODES, dtype=jnp.float32)
    reached = identity
    for repeat in range(NODES):
        reached = jnp.minimum(1.0, identity + jnp.dot(parent_hot, reached, precision=HIGHEST))
    return reached

def attend_request(operands):
    query, tree_pair, cache_pair, length, parent_row = operands
    group_size = HQ // KVH
    score_scale = 1.0 / math.sqrt(HD)
    heads = query.astype(jnp.float32).reshape(NODES, KVH, group_size, HD)
    cache_keys = cache_pair[0].astype(jnp.float32).reshape(CTX, KVH, HD)
    cache_values = cache_pair[1].astype(jnp.float32).reshape(CTX, KVH, HD)
    tree_keys = tree_pair[:, 0].astype(jnp.float32).reshape(NODES, KVH, HD)
    tree_values = tree_pair[:, 1].astype(jnp.float32).reshape(NODES, KVH, HD)
    cache_scores = jnp.einsum('nkgd,skd->kgns', heads, cache_keys, precision=HIGHEST) * score_scale
    tree_scores = jnp.einsum('nkgd,jkd->kgnj', heads, tree_keys, precision=HIGHEST) * score_scale
    scores = jnp.concatenate([cache_scores, tree_scores], axis=-1)
    cache_usable = jnp.arange(CTX, dtype=jnp.int32) < length
    tree_usable = reach_table(parent_row) > 0.5
    usable = jnp.concatenate([jnp.broadcast_to(cache_usable, (KVH, group_size, NODES, CTX)), jnp.broadcast_to(tree_usable, (KVH, group_size, NODES, NODES))], axis=-1)
    maxima = lax.optimization_barrier(jnp.max(jnp.where(usable, scores, FLOOR), axis=-1, keepdims=True))
    weights = jnp.where(usable, jnp.exp(scores - maxima), 0.0)
    totals = lax.optimization_barrier(jnp.sum(weights, axis=-1))
    rounded = lax.optimization_barrier(weights.astype(jnp.bfloat16)).astype(jnp.float32)
    summed = jnp.einsum('kgns,skd->nkgd', rounded[..., :CTX], cache_values, precision=HIGHEST)
    summed = summed + jnp.einsum('kgnj,jkd->nkgd', rounded[..., CTX:], tree_values, precision=HIGHEST)
    output = summed / jnp.transpose(totals, (2, 0, 1))[..., None]
    return output.reshape(NODES, HQ * HD).astype(jnp.bfloat16)

def blocked_sum(left, right, pieces):
    width = left.shape[1] // pieces

    def absorb(running, number):
        offset = (number * width).astype(jnp.int32)
        left_part = lax.dynamic_slice_in_dim(left, offset, width, 1)
        right_part = lax.dynamic_slice_in_dim(right, offset, width, 0)
        term = jnp.dot(left_part, right_part, preferred_element_type=jnp.float32)
        term = lax.optimization_barrier(term.astype(jnp.bfloat16)).astype(jnp.float32)
        return (running + term, None)
    initial = jnp.zeros((left.shape[0], right.shape[1]), jnp.float32)
    result, unused = lax.scan(absorb, initial, jnp.arange(pieces, dtype=jnp.int32))
    return result

def reference(queries, tree_kv, cache, ctx_len, parents, stream, out_weight, norm_gain, gate_weight, up_weight, down_weight):
    attention_rows = lax.map(attend_request, (queries, tree_kv, cache, ctx_len, parents))
    attention_rows = attention_rows.reshape(TOKENS, HQ * HD)
    projected = blocked_sum(attention_rows, out_weight, N_ROW)
    attended = (stream.astype(jnp.float32) + projected).astype(jnp.bfloat16)
    widened = attended.astype(jnp.float32)
    squares = lax.optimization_barrier(jnp.sum(widened * widened, axis=1))
    inverse = lax.rsqrt(squares / D + EPSILON)
    normed = (widened * inverse[:, None] * norm_gain).astype(jnp.bfloat16)
    gate = blocked_sum(normed, gate_weight, N_GRP * N_COL)
    upward = blocked_sum(normed, up_weight, N_GRP * N_COL)
    hidden = (jax.nn.silu(gate) * upward).astype(jnp.bfloat16)
    lowered = blocked_sum(hidden, down_weight, N_ROW)
    layer_output = (widened + lowered).astype(jnp.bfloat16)
    return (attended, layer_output)
```

```python
import functools
import math

import jax
import jax.numpy as jnp
from jax import lax
from jax.experimental import pallas as pl
from jax.experimental.pallas import tpu as pltpu
from jax.sharding import PartitionSpec as P

D = 8192
HD = 128
FLOOR = -1e30
EPSILON = 1e-05
PLANE = ("grp", "col")
LANES = 128
VMEM = pl.BlockSpec(memory_space=pltpu.VMEM)
SMEM = pl.BlockSpec(memory_space=pltpu.SMEM)
BF = jnp.bfloat16
F32 = jnp.float32


def call(kernel, out_shape, in_specs, flops, moved, **more):
    return pl.pallas_call(
        kernel,
        out_shape=out_shape,
        in_specs=in_specs,
        out_specs=more.pop("out_specs", jax.tree.map(lambda unused: VMEM, out_shape)),
        cost_estimate=pl.CostEstimate(flops=flops, bytes_accessed=moved, transcendentals=0),
        compiler_params=pltpu.CompilerParams(vmem_limit_bytes=32 * 1024 * 1024),
        **more,
    )


def shape(*dims, kind=BF):
    return jax.ShapeDtypeStruct(dims, kind)


def attend_kernel(copies, nodes, group, limit_ref, parents_ref, q_ref, tree_ref, cache_ref, out_ref):
    span = cache_ref.shape[2]
    rows = nodes * group
    scale = 1.0 / math.sqrt(HD)
    wide = q_ref[0].astype(F32)
    q = jnp.concatenate([wide[:, h * HD : (h + 1) * HD] for h in range(group)], axis=0).astype(BF)
    contract = (((1,), (1,)), ((), ()))
    scores = lax.dot_general(q, cache_ref[0, 0], contract, preferred_element_type=F32) * scale
    position = lax.broadcasted_iota(jnp.int32, (rows, span), 1)
    scores = jnp.where(position < limit_ref[0], scores, FLOOR)

    lane = lax.broadcasted_iota(jnp.int32, (nodes, nodes), 1)
    here = lax.broadcasted_iota(jnp.int32, (nodes, nodes), 0)
    reach = jnp.zeros((nodes, nodes), jnp.int32)
    for unused in range(nodes):
        reach = jnp.where(lane == here, 1, reach)
        above = jnp.full((nodes, nodes), -1, jnp.int32)
        for j in range(nodes):
            above = jnp.where(here == j, parents_ref[0, j], above)
        here = above
    reach = reach * limit_ref[1]
    reach = jnp.concatenate([reach] * group, axis=0)
    tree_keys = tree_ref[:, :HD]
    tree_values = tree_ref[:, HD:].astype(F32)
    tree_scores = lax.dot_general(q, tree_keys, contract, preferred_element_type=F32) * scale
    tree_scores = jnp.where(reach > 0, tree_scores, FLOOR)

    maxima = jnp.maximum(
        jnp.max(scores, axis=1, keepdims=True), jnp.max(tree_scores, axis=1, keepdims=True)
    )
    weights = jnp.exp(scores - maxima)
    tree_weights = jnp.exp(tree_scores - maxima)
    totals = jnp.sum(weights, axis=1, keepdims=True) + jnp.sum(tree_weights, axis=1, keepdims=True)
    summed = jnp.dot(weights.astype(BF), cache_ref[0, 1], preferred_element_type=F32)
    tree_rounded = tree_weights.astype(BF).astype(F32)
    for j in range(nodes):
        summed = summed + tree_rounded[:, j : j + 1] * tree_values[j : j + 1, :]
    heads = summed / totals
    level = maxima + jnp.log(totals)

    high = level.astype(BF).astype(F32)
    middle = (level - high).astype(BF).astype(F32)
    low = level - high - middle
    lanes = lax.broadcasted_iota(jnp.int32, (nodes, LANES), 1)
    tail = jnp.zeros((nodes, LANES), F32)
    for h in range(group):
        for k, part in enumerate((high, middle, low)):
            tail = jnp.where(lanes == k * group + h, part[h * nodes : (h + 1) * nodes], tail)
    line = jnp.concatenate(
        [heads[h * nodes : (h + 1) * nodes] for h in range(group)] + [tail], axis=1
    ).astype(BF)
    for k in range(copies):
        out_ref[k] = line


def join_kernel(cols, group, odd_ref, in_ref, out_ref):
    width = group * HD
    odd = odd_ref[0] > 0
    per_block = out_ref.shape[2] // HD
    block = []
    for c in range(cols):
        levels = []
        for g in range(2):
            tail = in_ref[g * cols + c, :, width:].astype(F32)
            levels.append(
                tail + jnp.roll(tail, -group, axis=1) + jnp.roll(tail, -2 * group, axis=1)
            )
        share = 1.0 / (1.0 + jnp.exp(levels[1] - levels[0]))
        rest = 1.0 / (1.0 + jnp.exp(levels[0] - levels[1]))
        for h in range(group):
            near = in_ref[c, :, h * HD : (h + 1) * HD].astype(F32)
            far = in_ref[cols + c, :, h * HD : (h + 1) * HD].astype(F32)
            block.append(near * share[:, h : h + 1] + far * rest[:, h : h + 1])
            if len(block) == per_block:
                half = per_block // 2
                first = jnp.concatenate(block[:half], axis=1)
                second = jnp.concatenate(block[half:], axis=1)
                mine = jnp.where(odd, second, first)
                other = jnp.where(odd, first, second)
                number = (c * group + h) // per_block
                out_ref[number] = jnp.concatenate([mine, other], axis=1).astype(BF)
                block = []


def project_kernel(a_ref, mine_ref, other_ref, out_ref):
    half = mine_ref.shape[0]
    out_ref[...] = (
        jnp.dot(a_ref[:, :half], mine_ref[...], preferred_element_type=F32)
        + jnp.dot(a_ref[:, half:], other_ref[...], preferred_element_type=F32)
    ).astype(BF)


def total(parts_ref):
    summed = parts_ref[0].astype(F32)
    for k in range(1, parts_ref.shape[0]):
        summed = summed + parts_ref[k].astype(F32)
    return summed


def residual_kernel(parts_ref, stream_ref, out_ref, copies_ref):
    attended = (stream_ref[...].astype(F32) + total(parts_ref)).astype(BF)
    out_ref[...] = attended
    for k in range(copies_ref.shape[0]):
        copies_ref[k] = attended


def final_kernel(parts_ref, attended_ref, out_ref):
    out_ref[...] = (attended_ref[...].astype(F32) + total(parts_ref)).astype(BF)


def widen_kernel(x_ref, gain_ref, gate_ref, up_ref, *rest):
    out_ref = rest[-1]
    units = gate_ref.shape[1]
    x = x_ref[...].astype(F32)
    squares = jnp.sum(x * x, axis=1, keepdims=True)
    scaled = (x * gain_ref[...]).astype(BF)
    out_ref[:, :units] = jnp.dot(scaled, gate_ref[...], preferred_element_type=F32).astype(BF)
    out_ref[:, units : 2 * units] = jnp.dot(
        scaled, up_ref[...], preferred_element_type=F32
    ).astype(BF)
    high = squares.astype(BF).astype(F32)
    lanes = lax.broadcasted_iota(jnp.int32, (x.shape[0], LANES), 1)
    tail = jnp.where(lanes == 0, high, jnp.where(lanes == 1, squares - high, 0.0))
    out_ref[:, 2 * units :] = tail.astype(BF)


def hidden_kernel(units, parts_ref, out_ref):
    sources = parts_ref.shape[0]

    def summed(start, size):
        return functools.reduce(
            lambda a, b: a + b,
            [parts_ref[k, :, start : start + size].astype(F32) for k in range(sources)],
        )

    squares = jnp.sum(summed(2 * units, LANES), axis=1, keepdims=True)
    inverse = lax.rsqrt(squares / D + EPSILON)
    for start in range(0, units, LANES):
        gate = summed(start, LANES) * inverse
        upward = summed(units + start, LANES) * inverse
        hidden = (gate / (1.0 + jnp.exp(-gate)) * upward).astype(BF)
        for k in range(out_ref.shape[0]):
            out_ref[k, :, start : start + LANES] = hidden


def lower_kernel(h_ref, weight_ref, out_ref):
    out_ref[...] = jnp.dot(h_ref[...], weight_ref[...], preferred_element_type=F32).astype(BF)


def lower_add_kernel(h_ref, weight_ref, other_ref, out_ref):
    out_ref[...] = (
        jnp.dot(h_ref[...], weight_ref[...], preferred_element_type=F32)
        + other_ref[...].astype(F32)
    ).astype(BF)


def on_device(
    queries,
    tree_kv,
    cache,
    ctx_len,
    parents,
    stream,
    out_weight,
    norm_gain,
    gate_weight,
    up_weight,
    down_weight,
):
    rows = lax.axis_size("row")
    cols = lax.axis_size("col")
    plane = lax.axis_size("grp") * cols
    chips = rows // 2
    ring = [[2 * z + core for z in range(chips)] for core in range(2)]
    swap = [(r, r ^ 1) for r in range(rows)]
    nodes = queries.shape[1]
    group = queries.shape[2] // HD
    span = cache.shape[2]
    local = out_weight.shape[1]
    units = gate_weight.shape[1]
    odd = (lax.axis_index("row") % 2).astype(jnp.int32).reshape(1)

    def swapped(x):
        return lax.ppermute(x, "row", swap)

    def along_ring(x):
        return lax.all_to_all(x, "row", 0, 0, axis_index_groups=ring, tiled=True)

    def in_plane(x):
        return lax.all_to_all(x, PLANE, 0, 0, tiled=True)

    other_weight = swapped(out_weight)

    last = lax.axis_index("grp") == lax.axis_size("grp") - 1
    limit = jnp.stack([ctx_len[0] - lax.axis_index("grp") * span, last.astype(jnp.int32)])
    tree = tree_kv.reshape(nodes, 2 * HD)
    width = group * HD
    lines = call(
        functools.partial(attend_kernel, plane, nodes, group),
        shape(plane, nodes, width + LANES),
        [SMEM, SMEM, VMEM, VMEM, VMEM],
        4 * nodes * group * span * HD,
        cache.size * 2,
    )(limit.astype(jnp.int32), parents, queries, tree, cache)
    lines = in_plane(lines)
    blocks = call(
        functools.partial(join_kernel, cols, group),
        shape(chips, nodes, D // chips),
        [SMEM, VMEM],
        4 * lines.size,
        lines.size * 2,
    )(odd, lines)
    tokens = chips * nodes
    portion = along_ring(blocks).reshape(tokens, D // chips)
    partial = call(
        project_kernel,
        shape(tokens, local),
        [VMEM, VMEM, VMEM],
        2 * tokens * local * (D // chips),
        out_weight.size * 4,
    )(portion, out_weight, other_weight)
    parts = along_ring(partial.reshape(chips, nodes, local))
    attended, copies = call(
        residual_kernel,
        (shape(nodes, local), shape(chips, nodes, local)),
        [VMEM, VMEM],
        parts.size,
        parts.size * 4,
    )(parts, stream)

    mine = along_ring(copies).reshape(tokens, local)
    other = swapped(mine)
    gain = norm_gain.reshape(1, local)
    wide = 2 * units + LANES
    flops = 4 * tokens * local * units
    first = call(
        widen_kernel,
        shape(2 * tokens, wide),
        [VMEM, VMEM, VMEM, VMEM],
        flops,
        gate_weight.size * 4,
        out_specs=pl.BlockSpec((tokens, wide), lambda i: (0, 0)),
        grid=(1,),
    )(mine, gain, gate_weight, up_weight)
    expanded = call(
        widen_kernel,
        shape(2 * tokens, wide),
        [VMEM, VMEM, VMEM, VMEM, pl.BlockSpec(memory_space=pl.ANY)],
        flops,
        gate_weight.size * 4,
        out_specs=pl.BlockSpec((tokens, wide), lambda i: (1, 0)),
        grid=(1,),
        input_output_aliases={4: 0},
    )(other, gain, gate_weight, up_weight, first)
    share = 2 * tokens // plane
    gathered = in_plane(expanded.reshape(plane, share, wide))
    hidden = call(
        functools.partial(hidden_kernel, units),
        shape(plane, share, units),
        [VMEM],
        gathered.size,
        gathered.size * 2,
    )(gathered)
    hidden = in_plane(hidden).reshape(2 * tokens, units)

    flops = 2 * tokens * local * units
    whole = pl.BlockSpec(down_weight.shape, lambda i: (0, 0))
    theirs = call(
        lower_kernel,
        shape(tokens, local),
        [pl.BlockSpec((tokens, units), lambda i: (1, 0)), whole],
        flops,
        down_weight.size * 2,
        grid=(1,),
        out_specs=pl.BlockSpec((tokens, local), lambda i: (0, 0)),
    )(hidden, down_weight)
    received = swapped(theirs)
    lowered = call(
        lower_add_kernel,
        shape(tokens, local),
        [
            pl.BlockSpec((tokens, units), lambda i: (0, 0)),
            whole,
            pl.BlockSpec((tokens, local), lambda i: (0, 0)),
        ],
        flops,
        down_weight.size * 2,
        grid=(1,),
        out_specs=pl.BlockSpec((tokens, local), lambda i: (0, 0)),
    )(hidden, down_weight, received)
    parts = along_ring(lowered.reshape(chips, nodes, local))
    layer_output = call(
        final_kernel, shape(nodes, local), [VMEM, VMEM], parts.size, parts.size * 2
    )(parts, attended)
    return (attended, layer_output)


def solution(mesh):
    placed = (
        P("row", None, "col"),
        P("row", None, None, "col"),
        P("row", None, "grp", "col"),
        P("row"),
        P("row", None),
        P("row", ("grp", "col")),
        P("row", ("grp", "col")),
        P(("grp", "col")),
        P(("grp", "col"), "row"),
        P(("grp", "col"), "row"),
        P("row", ("grp", "col")),
    )
    return jax.shard_map(
        on_device,
        mesh=mesh,
        in_specs=placed,
        out_specs=(P("row", ("grp", "col")), P("row", ("grp", "col"))),
        check_vma=False,
    )
```

```python
import functools
import math

import jax
import jax.numpy as jnp
from jax import lax
from jax.experimental import pallas as pl
from jax.experimental.pallas import tpu as pltpu
from jax.sharding import PartitionSpec as P

D = 8192
HD = 128
FLOOR = -1e30
EPSILON = 1e-05
PLANE = ("grp", "col")
LANES = 128
VMEM = pl.BlockSpec(memory_space=pltpu.VMEM)
SMEM = pl.BlockSpec(memory_space=pltpu.SMEM)
BF = jnp.bfloat16
F32 = jnp.float32


def call(kernel, out_shape, in_specs, flops, moved, **more):
    return pl.pallas_call(
        kernel,
        out_shape=out_shape,
        in_specs=in_specs,
        out_specs=more.pop("out_specs", jax.tree.map(lambda unused: VMEM, out_shape)),
        cost_estimate=pl.CostEstimate(flops=flops, bytes_accessed=moved, transcendentals=0),
        compiler_params=pltpu.CompilerParams(vmem_limit_bytes=16 * 1024 * 1024),
        **more,
    )


def shape(*dims, kind=BF):
    return jax.ShapeDtypeStruct(dims, kind)


def attend_kernel(copies, nodes, group, limit_ref, parents_ref, q_ref, tree_ref, cache_ref, out_ref):
    span = cache_ref.shape[2]
    rows = nodes * group
    scale = 1.0 / math.sqrt(HD)
    wide = q_ref[0].astype(F32)
    q = jnp.concatenate([wide[:, h * HD : (h + 1) * HD] for h in range(group)], axis=0).astype(BF)
    contract = (((1,), (1,)), ((), ()))
    scores = lax.dot_general(q, cache_ref[0, 0], contract, preferred_element_type=F32) * scale
    position = lax.broadcasted_iota(jnp.int32, (rows, span), 1)
    scores = jnp.where(position < limit_ref[0], scores, FLOOR)

    lane = lax.broadcasted_iota(jnp.int32, (nodes, nodes), 1)
    here = lax.broadcasted_iota(jnp.int32, (nodes, nodes), 0)
    reach = jnp.zeros((nodes, nodes), jnp.int32)
    for unused in range(nodes):
        reach = jnp.where(lane == here, 1, reach)
        above = jnp.full((nodes, nodes), -1, jnp.int32)
        for j in range(nodes):
            above = jnp.where(here == j, parents_ref[0, j], above)
        here = above
    reach = reach * limit_ref[1]
    reach = jnp.concatenate([reach] * group, axis=0)
    tree_keys = tree_ref[:, :HD]
    tree_values = tree_ref[:, HD:].astype(F32)
    tree_scores = lax.dot_general(q, tree_keys, contract, preferred_element_type=F32) * scale
    tree_scores = jnp.where(reach > 0, tree_scores, FLOOR)

    maxima = jnp.maximum(
        jnp.max(scores, axis=1, keepdims=True), jnp.max(tree_scores, axis=1, keepdims=True)
    )
    weights = jnp.exp(scores - maxima)
    tree_weights = jnp.exp(tree_scores - maxima)
    totals = jnp.sum(weights, axis=1, keepdims=True) + jnp.sum(tree_weights, axis=1, keepdims=True)
    summed = jnp.dot(weights.astype(BF), cache_ref[0, 1], preferred_element_type=F32)
    tree_rounded = tree_weights.astype(BF).astype(F32)
    for j in range(nodes):
        summed = summed + tree_rounded[:, j : j + 1] * tree_values[j : j + 1, :]
    heads = summed / totals
    level = maxima + jnp.log(totals)

    high = level.astype(BF).astype(F32)
    middle = (level - high).astype(BF).astype(F32)
    low = level - high - middle
    lanes = lax.broadcasted_iota(jnp.int32, (nodes, LANES), 1)
    tail = jnp.zeros((nodes, LANES), F32)
    for h in range(group):
        for k, part in enumerate((high, middle, low)):
            tail = jnp.where(lanes == k * group + h, part[h * nodes : (h + 1) * nodes], tail)
    line = jnp.concatenate(
        [heads[h * nodes : (h + 1) * nodes] for h in range(group)] + [tail], axis=1
    ).astype(BF)
    for k in range(copies):
        out_ref[k] = line


def join_kernel(cols, group, sources, targets, odd_ref, in_ref, out_ref):
    width = group * HD
    odd = odd_ref[0] > 0
    per_block = out_ref.shape[2] // HD
    block = []
    for c in range(cols):
        levels = []
        for g in range(2):
            tail = in_ref[sources.index(g * cols + c), :, width:].astype(F32)
            levels.append(
                tail + jnp.roll(tail, -group, axis=1) + jnp.roll(tail, -2 * group, axis=1)
            )
        share = 1.0 / (1.0 + jnp.exp(levels[1] - levels[0]))
        for h in range(group):
            near = in_ref[sources.index(c), :, h * HD : (h + 1) * HD].astype(F32)
            far = in_ref[sources.index(cols + c), :, h * HD : (h + 1) * HD].astype(F32)
            block.append(far + (near - far) * share[:, h : h + 1])
            if len(block) == per_block:
                half = per_block // 2
                first = jnp.concatenate(block[:half], axis=1)
                second = jnp.concatenate(block[half:], axis=1)
                mine = jnp.where(odd, second, first)
                other = jnp.where(odd, first, second)
                number = (c * group + h) // per_block
                out_ref[targets.index(number)] = jnp.concatenate([mine, other], axis=1).astype(BF)
                block = []


def project_kernel(a_ref, mine_ref, other_ref, out_ref):
    half = mine_ref.shape[0]
    out_ref[...] = (
        jnp.dot(a_ref[:, :half], mine_ref[...], preferred_element_type=F32)
        + jnp.dot(a_ref[:, half:], other_ref[...], preferred_element_type=F32)
    ).astype(BF)


def total(parts_ref):
    summed = parts_ref[0].astype(F32)
    for k in range(1, parts_ref.shape[0]):
        summed = summed + parts_ref[k].astype(F32)
    return summed


def residual_kernel(parts_ref, stream_ref, out_ref, copies_ref):
    attended = (stream_ref[...].astype(F32) + total(parts_ref)).astype(BF)
    out_ref[...] = attended
    for k in range(copies_ref.shape[0]):
        copies_ref[k] = attended


def final_kernel(parts_ref, attended_ref, out_ref):
    out_ref[...] = (attended_ref[...].astype(F32) + total(parts_ref)).astype(BF)


def widen_kernel(x_ref, gain_ref, *rest):
    weights, out_ref = rest[:-1], rest[-1]
    units = weights[0].shape[1]
    x = x_ref[...].astype(F32)
    squares = jnp.sum(x * x, axis=1, keepdims=True)
    scaled = (x * gain_ref[...]).astype(BF)
    for k, weight_ref in enumerate(weights):
        out_ref[:, k * units : (k + 1) * units] = jnp.dot(
            scaled, weight_ref[...], preferred_element_type=F32
        ).astype(BF)
    high = squares.astype(BF).astype(F32)
    lanes = lax.broadcasted_iota(jnp.int32, (x.shape[0], LANES), 1)
    tail = jnp.where(lanes == 0, high, jnp.where(lanes == 1, squares - high, 0.0))
    out_ref[:, len(weights) * units :] = tail.astype(BF)


def hidden_kernel(units, parts_ref, out_ref):
    sources = parts_ref.shape[0]

    def summed(start, size):
        return functools.reduce(
            lambda a, b: a + b,
            [parts_ref[k, :, start : start + size].astype(F32) for k in range(sources)],
        )

    squares = jnp.sum(summed(2 * units, LANES), axis=1, keepdims=True)
    inverse = lax.rsqrt(squares / D + EPSILON)
    for start in range(0, units, LANES):
        gate = summed(start, LANES) * inverse
        upward = summed(units + start, LANES) * inverse
        hidden = (gate / (1.0 + jnp.exp(-gate)) * upward).astype(BF)
        for k in range(out_ref.shape[0]):
            out_ref[k, :, start : start + LANES] = hidden


def on_device(
    queries,
    tree_kv,
    cache,
    ctx_len,
    parents,
    stream,
    out_weight,
    norm_gain,
    gate_weight,
    up_weight,
    down_weight,
):
    rows = lax.axis_size("row")
    cols = lax.axis_size("col")
    plane = lax.axis_size("grp") * cols
    chips = rows // 2
    far = chips // 2
    targets = [(z + far) % chips for z in range(chips)]
    ring = [[2 * z + core for z in targets] for core in range(2)]
    sources = [(p + 12) % plane for p in range(plane)]
    swap = [(r, r ^ 1) for r in range(rows)]
    nodes = queries.shape[1]
    group = queries.shape[2] // HD
    span = cache.shape[2]
    local = out_weight.shape[1]
    units = gate_weight.shape[1]
    odd = (lax.axis_index("row") % 2).astype(jnp.int32).reshape(1)

    def swapped(x):
        return lax.ppermute(x, "row", swap)

    def along_ring(x):
        return lax.all_to_all(x, "row", 0, 0, axis_index_groups=ring, tiled=True)

    def in_plane(x):
        return lax.all_to_all(x, PLANE, 0, 0, axis_index_groups=[sources], tiled=True)

    other_weight = swapped(out_weight)
    other_gate = swapped(gate_weight)
    other_up = swapped(up_weight)
    other_down = swapped(down_weight)

    last = lax.axis_index("grp") == lax.axis_size("grp") - 1
    limit = jnp.stack([ctx_len[0] - lax.axis_index("grp") * span, last.astype(jnp.int32)])
    tree = tree_kv.reshape(nodes, 2 * HD)
    width = group * HD
    lines = call(
        functools.partial(attend_kernel, plane, nodes, group),
        shape(plane, nodes, width + LANES),
        [SMEM, SMEM, VMEM, VMEM, VMEM],
        4 * nodes * group * span * HD,
        cache.size * 2,
    )(limit.astype(jnp.int32), parents, queries, tree, cache)
    lines = in_plane(lines)
    blocks = call(
        functools.partial(join_kernel, cols, group, sources, targets),
        shape(chips, nodes, D // chips),
        [SMEM, VMEM],
        4 * lines.size,
        lines.size * 2,
    )(odd, lines)
    tokens = chips * nodes
    portion = along_ring(blocks).reshape(tokens, D // chips)
    partial = call(
        project_kernel,
        shape(tokens, local),
        [VMEM, VMEM, VMEM],
        2 * tokens * local * (D // chips),
        out_weight.size * 4,
    )(portion, out_weight, other_weight)
    parts = along_ring(partial.reshape(chips, nodes, local))
    attended, copies = call(
        residual_kernel,
        (shape(nodes, local), shape(chips, nodes, local)),
        [VMEM, VMEM],
        parts.size,
        parts.size * 4,
    )(parts, stream)

    mine = along_ring(copies).reshape(tokens, local)
    wide = 4 * units + LANES
    expanded = call(
        widen_kernel,
        shape(tokens, wide),
        [VMEM] * 6,
        8 * tokens * local * units,
        gate_weight.size * 8,
    )(mine, norm_gain.reshape(1, local), gate_weight, other_gate, up_weight, other_up)
    share = tokens // plane
    gathered = in_plane(expanded.reshape(plane, share, wide))
    hidden = call(
        functools.partial(hidden_kernel, 2 * units),
        shape(plane, share, 2 * units),
        [VMEM],
        gathered.size,
        gathered.size * 2,
    )(gathered)
    hidden = in_plane(hidden).reshape(tokens, 2 * units)
    lowered = call(
        project_kernel,
        shape(tokens, local),
        [VMEM, VMEM, VMEM],
        4 * tokens * local * units,
        down_weight.size * 4,
    )(hidden, down_weight, other_down)
    parts = along_ring(lowered.reshape(chips, nodes, local))
    layer_output = call(
        final_kernel, shape(nodes, local), [VMEM, VMEM], parts.size, parts.size * 2
    )(parts, attended)
    return (attended, layer_output)


def solution(mesh):
    placed = (
        P("row", None, "col"),
        P("row", None, None, "col"),
        P("row", None, "grp", "col"),
        P("row"),
        P("row", None),
        P("row", ("grp", "col")),
        P("row", ("grp", "col")),
        P(("grp", "col")),
        P(("grp", "col"), "row"),
        P(("grp", "col"), "row"),
        P("row", ("grp", "col")),
    )
    return jax.shard_map(
        on_device,
        mesh=mesh,
        in_specs=placed,
        out_specs=(P("row", ("grp", "col")), P("row", ("grp", "col"))),
        check_vma=False,
    )
```

```python
import functools
import math

import jax
import jax.numpy as jnp
from jax import lax
from jax.experimental import pallas as pl
from jax.experimental.pallas import tpu as pltpu
from jax.sharding import PartitionSpec as P

D = 8192
HD = 128
FLOOR = -1e30
EPSILON = 1e-05
PLANE = ("grp", "col")
LANES = 128
VMEM = pl.BlockSpec(memory_space=pltpu.VMEM)
SMEM = pl.BlockSpec(memory_space=pltpu.SMEM)
ANY = pl.BlockSpec(memory_space=pl.ANY)
HBM = pl.BlockSpec(memory_space=pltpu.HBM)
BF = jnp.bfloat16
F32 = jnp.float32


def call(kernel, out_shape, in_specs, flops, moved, **more):
    return pl.pallas_call(
        kernel,
        out_shape=out_shape,
        in_specs=in_specs,
        out_specs=more.pop("out_specs", jax.tree.map(lambda unused: VMEM, out_shape)),
        cost_estimate=pl.CostEstimate(flops=flops, bytes_accessed=moved, transcendentals=0),
        compiler_params=pltpu.CompilerParams(vmem_limit_bytes=more.pop("vmem", 16) * 1024 * 1024),
        **more,
    )


def shape(*dims, kind=BF):
    return jax.ShapeDtypeStruct(dims, kind)


def attend_kernel(
    nodes,
    group,
    pieces,
    length_ref,
    parents_ref,
    q_ref,
    tree_ref,
    cache_ref,
    out_ref,
    length,
    parents,
    q_wide,
    tree_pair,
    cached,
    sems,
    cache_sems,
):
    span = cache_ref.shape[2]
    rows = nodes * group
    scale = 1.0 / math.sqrt(HD)
    small = [
        pltpu.make_async_copy(source, target, sems.at[k])
        for k, (source, target) in enumerate(
            [(q_ref, q_wide), (length_ref, length), (parents_ref, parents), (tree_ref, tree_pair)]
        )
    ]
    size = span // pieces
    large = [
        pltpu.make_async_copy(
            cache_ref.at[0, part, pl.ds(k * size, size)],
            cached.at[part, pl.ds(k * size, size)],
            cache_sems.at[part, k],
        )
        for part in range(2)
        for k in range(pieces)
    ]
    for copy in small + large:
        copy.start()
    for copy in small:
        copy.wait()
    place = lax.axis_index("grp")
    limit = length[0, 0] - place * span
    tree_here = (place == lax.axis_size("grp") - 1).astype(jnp.int32)

    wide = q_wide[0].astype(F32)
    q = jnp.concatenate([wide[:, h * HD : (h + 1) * HD] for h in range(group)], axis=0).astype(BF)
    contract = (((1,), (1,)), ((), ()))

    lane = lax.broadcasted_iota(jnp.int32, (nodes, nodes), 1)
    here = lax.broadcasted_iota(jnp.int32, (nodes, nodes), 0)
    reach = jnp.zeros((nodes, nodes), jnp.int32)
    for unused in range(nodes):
        reach = jnp.where(lane == here, 1, reach)
        above = jnp.full((nodes, nodes), -1, jnp.int32)
        for j in range(nodes):
            above = jnp.where(here == j, parents[0, j], above)
        here = above
    reach = jnp.concatenate([reach * tree_here] * group, axis=0)
    pair = tree_pair[0].astype(F32)
    tree_keys = pair[:, 0, :].astype(BF)
    tree_values = pair[:, 1, :]
    tree_scores = lax.dot_general(q, tree_keys, contract, preferred_element_type=F32) * scale
    tree_scores = jnp.where(reach > 0, tree_scores, FLOOR)
    maxima = jnp.max(tree_scores, axis=1, keepdims=True)

    for copy in large[:pieces]:
        copy.wait()
    scores = lax.dot_general(q, cached[0], contract, preferred_element_type=F32) * scale
    position = lax.broadcasted_iota(jnp.int32, (rows, span), 1)
    scores = jnp.where(position < limit, scores, FLOOR)
    maxima = jnp.maximum(maxima, jnp.max(scores, axis=1, keepdims=True))
    tree_weights = jnp.exp(tree_scores - maxima)
    totals = jnp.sum(tree_weights, axis=1, keepdims=True)
    tree_rounded = tree_weights.astype(BF).astype(F32)
    summed = jnp.zeros((rows, HD), F32)
    for j in range(nodes):
        summed = summed + tree_rounded[:, j : j + 1] * tree_values[j : j + 1, :]
    weights = jnp.exp(scores - maxima)
    totals = totals + jnp.sum(weights, axis=1, keepdims=True)
    for copy in large[pieces:]:
        copy.wait()
    summed = summed + jnp.dot(weights.astype(BF), cached[1], preferred_element_type=F32)
    heads = summed / totals
    level = maxima + jnp.log(totals)

    high = level.astype(BF).astype(F32)
    middle = (level - high).astype(BF).astype(F32)
    low = level - high - middle
    lanes = lax.broadcasted_iota(jnp.int32, (nodes, LANES), 1)
    tail = jnp.zeros((nodes, LANES), F32)
    for h in range(group):
        for k, part in enumerate((high, middle, low)):
            tail = jnp.where(lanes == k * group + h, part[h * nodes : (h + 1) * nodes], tail)
    line = jnp.concatenate(
        [heads[h * nodes : (h + 1) * nodes] for h in range(group)] + [tail], axis=1
    ).astype(BF)
    for k in range(out_ref.shape[0]):
        out_ref[k] = line


def join_kernel(cols, group, sources, targets, odd_ref, in_ref, out_ref):
    width = group * HD
    odd = odd_ref[0] > 0
    per_block = out_ref.shape[2] // HD
    block = []
    for c in range(cols):
        levels = []
        for g in range(2):
            tail = in_ref[sources.index(g * cols + c), :, width:].astype(F32)
            levels.append(
                tail + jnp.roll(tail, -group, axis=1) + jnp.roll(tail, -2 * group, axis=1)
            )
        share = 1.0 / (1.0 + jnp.exp(levels[1] - levels[0]))
        for h in range(group):
            near = in_ref[sources.index(c), :, h * HD : (h + 1) * HD].astype(F32)
            far = in_ref[sources.index(cols + c), :, h * HD : (h + 1) * HD].astype(F32)
            block.append(far + (near - far) * share[:, h : h + 1])
            if len(block) == per_block:
                half = per_block // 2
                first = jnp.concatenate(block[:half], axis=1)
                second = jnp.concatenate(block[half:], axis=1)
                mine = jnp.where(odd, second, first)
                other = jnp.where(odd, first, second)
                number = (c * group + h) // per_block
                out_ref[targets.index(number)] = jnp.concatenate([mine, other], axis=1).astype(BF)
                block = []


def project_kernel(a_ref, mine_ref, other_ref, out_ref):
    half = mine_ref.shape[0]
    out_ref[...] = (
        jnp.dot(a_ref[:, :half], mine_ref[...], preferred_element_type=F32)
        + jnp.dot(a_ref[:, half:], other_ref[...], preferred_element_type=F32)
    ).astype(BF)


def total(parts_ref):
    summed = parts_ref[0].astype(F32)
    for k in range(1, parts_ref.shape[0]):
        summed = summed + parts_ref[k].astype(F32)
    return summed


def residual_kernel(parts_ref, stream_ref, out_ref, copies_ref):
    attended = (stream_ref[...].astype(F32) + total(parts_ref)).astype(BF)
    out_ref[...] = attended
    for k in range(copies_ref.shape[0]):
        copies_ref[k] = attended


def final_kernel(parts_ref, attended_ref, out_ref):
    out_ref[...] = (attended_ref[...].astype(F32) + total(parts_ref)).astype(BF)


def widen_kernel(x_ref, gain_ref, *rest):
    weights, (out_ref, held, sems) = rest[:4], rest[4:]
    units = weights[0].shape[1]
    size = held.shape[1] // sems.shape[1]
    arriving = [
        [
            pltpu.make_async_copy(
                weights[k + 1].at[pl.ds(j * size, size)],
                held.at[k, pl.ds(j * size, size)],
                sems.at[k, j],
            )
            for j in range(sems.shape[1])
        ]
        for k in range(held.shape[0])
    ]
    for copies in arriving:
        for copy in copies:
            copy.start()
    x = x_ref[...].astype(F32)
    scaled = (x * gain_ref[...]).astype(BF)
    squares = jnp.sum(x * x, axis=1, keepdims=True)
    high = squares.astype(BF).astype(F32)
    lanes = lax.broadcasted_iota(jnp.int32, (x.shape[0], LANES), 1)
    tail = jnp.where(lanes == 0, high, jnp.where(lanes == 1, squares - high, 0.0))
    out_ref[:, 4 * units :] = tail.astype(BF)
    for k in range(4):
        if k > 0:
            for copy in arriving[k - 1]:
                copy.wait()
        weight = weights[0][...] if k == 0 else held[k - 1]
        out_ref[:, k * units : (k + 1) * units] = jnp.dot(
            scaled, weight, preferred_element_type=F32
        ).astype(BF)


def hidden_kernel(units, parts_ref, out_ref):
    sources = parts_ref.shape[0]

    def summed(start, size):
        return functools.reduce(
            lambda a, b: a + b,
            [parts_ref[k, :, start : start + size].astype(F32) for k in range(sources)],
        )

    squares = jnp.sum(summed(2 * units, LANES), axis=1, keepdims=True)
    inverse = lax.rsqrt(squares / D + EPSILON)
    for start in range(0, units, LANES):
        gate = summed(start, LANES) * inverse
        upward = summed(units + start, LANES) * inverse
        hidden = (gate / (1.0 + jnp.exp(-gate)) * upward).astype(BF)
        for k in range(out_ref.shape[0]):
            out_ref[k, :, start : start + LANES] = hidden


def on_device(
    queries,
    tree_kv,
    cache,
    ctx_len,
    parents,
    stream,
    out_weight,
    norm_gain,
    gate_weight,
    up_weight,
    down_weight,
):
    rows = lax.axis_size("row")
    cols = lax.axis_size("col")
    plane = lax.axis_size("grp") * cols
    chips = rows // 2
    far = chips // 2
    targets = [(z + far) % chips for z in range(chips)]
    ring = [[2 * z + core for z in targets] for core in range(2)]
    sources = [(p + 12) % plane for p in range(plane)]
    swap = [(r, r ^ 1) for r in range(rows)]
    nodes = queries.shape[1]
    group = queries.shape[2] // HD
    span = cache.shape[2]
    local = out_weight.shape[1]
    units = gate_weight.shape[1]
    odd = (lax.axis_index("row") % 2).astype(jnp.int32).reshape(1)

    def swapped(x):
        return lax.ppermute(x, "row", swap)

    def along_ring(x):
        return lax.all_to_all(x, "row", 0, 0, axis_index_groups=ring, tiled=True)

    def in_plane(x):
        return lax.all_to_all(x, PLANE, 0, 0, axis_index_groups=[sources], tiled=True)

    other_weight = swapped(out_weight)
    other_gate = swapped(gate_weight)
    other_up = swapped(up_weight)
    other_down = swapped(down_weight)

    width = group * HD
    pieces = 2
    lines = call(
        functools.partial(attend_kernel, nodes, group, pieces),
        shape(plane, nodes, width + LANES),
        [ANY] * 5,
        4 * nodes * group * span * HD,
        cache.size * 2,
        scratch_shapes=[
            pltpu.SMEM((1, 1), jnp.int32),
            pltpu.SMEM(parents.shape, jnp.int32),
            pltpu.VMEM(queries.shape, BF),
            pltpu.VMEM(tree_kv.shape, BF),
            pltpu.VMEM(cache.shape[1:], BF),
            pltpu.SemaphoreType.DMA((4,)),
            pltpu.SemaphoreType.DMA((2, pieces)),
        ],
        vmem=56,
    )(ctx_len.reshape(1, 1), parents, queries, tree_kv, cache)
    lines, other_weight = lax.optimization_barrier((in_plane(lines), other_weight))
    blocks = call(
        functools.partial(join_kernel, cols, group, sources, targets),
        shape(chips, nodes, D // chips),
        [SMEM, VMEM],
        4 * lines.size,
        lines.size * 2,
    )(odd, lines)
    tokens = chips * nodes
    portion = along_ring(blocks).reshape(tokens, D // chips)
    partial = call(
        project_kernel,
        shape(tokens, local),
        [VMEM, VMEM, VMEM],
        2 * tokens * local * (D // chips),
        out_weight.size * 4,
    )(portion, out_weight, other_weight)
    parts, other_gate, other_up = lax.optimization_barrier(
        (along_ring(partial.reshape(chips, nodes, local)), other_gate, other_up)
    )
    attended, copies = call(
        residual_kernel,
        (shape(nodes, local), shape(chips, nodes, local)),
        [VMEM, VMEM],
        parts.size,
        parts.size * 4,
    )(parts, stream)

    mine, other_down = lax.optimization_barrier((along_ring(copies), other_down))
    mine = mine.reshape(tokens, local)
    wide = 4 * units + LANES
    expanded = call(
        widen_kernel,
        shape(tokens, wide),
        [VMEM] * 3 + [HBM] * 3,
        8 * tokens * local * units,
        gate_weight.size * 8,
        scratch_shapes=[
            pltpu.VMEM((3,) + up_weight.shape, BF),
            pltpu.SemaphoreType.DMA((3, 2)),
        ],
    )(mine, norm_gain.reshape(1, local), gate_weight, other_gate, up_weight, other_up)
    share = tokens // plane
    gathered = in_plane(expanded.reshape(plane, share, wide))
    hidden = call(
        functools.partial(hidden_kernel, 2 * units),
        shape(plane, share, 2 * units),
        [VMEM],
        gathered.size,
        gathered.size * 2,
    )(gathered)
    hidden = in_plane(hidden).reshape(tokens, 2 * units)
    lowered = call(
        project_kernel,
        shape(tokens, local),
        [VMEM, VMEM, VMEM],
        4 * tokens * local * units,
        down_weight.size * 4,
    )(hidden, down_weight, other_down)
    parts = along_ring(lowered.reshape(chips, nodes, local))
    layer_output = call(
        final_kernel, shape(nodes, local), [VMEM, VMEM], parts.size, parts.size * 2
    )(parts, attended)
    return (attended, layer_output)


def solution(mesh):
    placed = (
        P("row", None, "col"),
        P("row", None, None, "col"),
        P("row", None, "grp", "col"),
        P("row"),
        P("row", None),
        P("row", ("grp", "col")),
        P("row", ("grp", "col")),
        P(("grp", "col")),
        P(("grp", "col"), "row"),
        P(("grp", "col"), "row"),
        P("row", ("grp", "col")),
    )
    return jax.shard_map(
        on_device,
        mesh=mesh,
        in_specs=placed,
        out_specs=(P("row", ("grp", "col")), P("row", ("grp", "col"))),
        check_vma=False,
    )
```

```python
import functools
import math

import jax
import jax.numpy as jnp
from jax import lax
from jax.experimental import pallas as pl
from jax.experimental.pallas import tpu as pltpu
from jax.sharding import PartitionSpec as P

D = 8192
HD = 128
FLOOR = -1e30
EPSILON = 1e-05
PLANE = ("grp", "col")
LANES = 128
VMEM = pl.BlockSpec(memory_space=pltpu.VMEM)
SMEM = pl.BlockSpec(memory_space=pltpu.SMEM)
ANY = pl.BlockSpec(memory_space=pl.ANY)
HBM = pl.BlockSpec(memory_space=pltpu.HBM)
BF = jnp.bfloat16
F32 = jnp.float32


def call(kernel, out_shape, in_specs, flops, moved, **more):
    return pl.pallas_call(
        kernel,
        out_shape=out_shape,
        in_specs=in_specs,
        out_specs=more.pop("out_specs", jax.tree.map(lambda unused: VMEM, out_shape)),
        cost_estimate=pl.CostEstimate(flops=flops, bytes_accessed=moved, transcendentals=0),
        compiler_params=pltpu.CompilerParams(vmem_limit_bytes=more.pop("vmem", 16) * 1024 * 1024),
        **more,
    )


def shape(*dims, kind=BF):
    return jax.ShapeDtypeStruct(dims, kind)


def attend_kernel(
    nodes,
    group,
    pieces,
    length_ref,
    parents_ref,
    q_ref,
    tree_ref,
    cache_ref,
    out_ref,
    length,
    parents,
    q_wide,
    tree_pair,
    cached,
    sems,
    cache_sems,
):
    span = cache_ref.shape[2]
    rows = nodes * group
    scale = 1.0 / math.sqrt(HD)
    small = [
        pltpu.make_async_copy(source, target, sems.at[k])
        for k, (source, target) in enumerate(
            [(q_ref, q_wide), (length_ref, length), (parents_ref, parents), (tree_ref, tree_pair)]
        )
    ]
    size = span // pieces
    large = [
        pltpu.make_async_copy(
            cache_ref.at[0, part, pl.ds(k * size, size)],
            cached.at[part, pl.ds(k * size, size)],
            cache_sems.at[part, k],
        )
        for part in range(2)
        for k in range(pieces)
    ]
    for copy in large[:pieces] + small + large[pieces:]:
        copy.start()
    for copy in small:
        copy.wait()
    place = lax.axis_index("grp")
    limit = length[0, 0] - place * span
    tree_here = (place == lax.axis_size("grp") - 1).astype(jnp.int32)

    wide = q_wide[0].astype(F32)
    q = jnp.concatenate([wide[:, h * HD : (h + 1) * HD] for h in range(group)], axis=0).astype(BF)
    contract = (((1,), (1,)), ((), ()))

    lane = lax.broadcasted_iota(jnp.int32, (nodes, nodes), 1)
    here = lax.broadcasted_iota(jnp.int32, (nodes, nodes), 0)
    reach = jnp.zeros((nodes, nodes), jnp.int32)
    for unused in range(nodes):
        reach = jnp.where(lane == here, 1, reach)
        above = jnp.full((nodes, nodes), -1, jnp.int32)
        for j in range(nodes):
            above = jnp.where(here == j, parents[0, j], above)
        here = above
    reach = jnp.concatenate([reach * tree_here] * group, axis=0)
    pair = tree_pair[0].astype(F32)
    tree_keys = pair[:, 0, :].astype(BF)
    tree_values = pair[:, 1, :]
    tree_scores = lax.dot_general(q, tree_keys, contract, preferred_element_type=F32) * scale
    tree_scores = jnp.where(reach > 0, tree_scores, FLOOR)
    maxima = jnp.max(tree_scores, axis=1, keepdims=True)

    for copy in large[:pieces]:
        copy.wait()
    scores = lax.dot_general(q, cached[0], contract, preferred_element_type=F32) * scale
    position = lax.broadcasted_iota(jnp.int32, (rows, span), 1)
    scores = jnp.where(position < limit, scores, FLOOR)
    maxima = jnp.maximum(maxima, jnp.max(scores, axis=1, keepdims=True))
    tree_weights = jnp.exp(tree_scores - maxima)
    totals = jnp.sum(tree_weights, axis=1, keepdims=True)
    tree_rounded = tree_weights.astype(BF).astype(F32)
    summed = jnp.zeros((rows, HD), F32)
    for j in range(nodes):
        summed = summed + tree_rounded[:, j : j + 1] * tree_values[j : j + 1, :]
    weights = jnp.exp(scores - maxima)
    totals = totals + jnp.sum(weights, axis=1, keepdims=True)
    for copy in large[pieces:]:
        copy.wait()
    summed = summed + jnp.dot(weights.astype(BF), cached[1], preferred_element_type=F32)
    heads = summed / totals
    level = maxima + jnp.log(totals)

    high = level.astype(BF).astype(F32)
    middle = (level - high).astype(BF).astype(F32)
    low = level - high - middle
    lanes = lax.broadcasted_iota(jnp.int32, (nodes, LANES), 1)
    tail = jnp.zeros((nodes, LANES), F32)
    for h in range(group):
        for k, part in enumerate((high, middle, low)):
            tail = jnp.where(lanes == k * group + h, part[h * nodes : (h + 1) * nodes], tail)
    line = jnp.concatenate(
        [heads[h * nodes : (h + 1) * nodes] for h in range(group)] + [tail], axis=1
    ).astype(BF)
    for k in range(out_ref.shape[0]):
        out_ref[k] = line


def join_kernel(cols, group, sources, targets, odd_ref, in_ref, out_ref):
    width = group * HD
    odd = odd_ref[0] > 0
    per_block = out_ref.shape[2] // HD
    block = []
    for c in range(cols):
        levels = []
        for g in range(2):
            tail = in_ref[sources.index(g * cols + c), :, width:].astype(F32)
            levels.append(
                tail + jnp.roll(tail, -group, axis=1) + jnp.roll(tail, -2 * group, axis=1)
            )
        share = 1.0 / (1.0 + jnp.exp(levels[1] - levels[0]))
        for h in range(group):
            near = in_ref[sources.index(c), :, h * HD : (h + 1) * HD].astype(F32)
            far = in_ref[sources.index(cols + c), :, h * HD : (h + 1) * HD].astype(F32)
            block.append(far + (near - far) * share[:, h : h + 1])
            if len(block) == per_block:
                half = per_block // 2
                first = jnp.concatenate(block[:half], axis=1)
                second = jnp.concatenate(block[half:], axis=1)
                mine = jnp.where(odd, second, first)
                other = jnp.where(odd, first, second)
                number = (c * group + h) // per_block
                out_ref[targets.index(number)] = jnp.concatenate([mine, other], axis=1).astype(BF)
                block = []


def project_kernel(a_ref, mine_ref, other_ref, out_ref):
    half = mine_ref.shape[0]
    out_ref[...] = (
        jnp.dot(a_ref[:, :half], mine_ref[...], preferred_element_type=F32)
        + jnp.dot(a_ref[:, half:], other_ref[...], preferred_element_type=F32)
    ).astype(BF)


def total(parts_ref):
    summed = parts_ref[0].astype(F32)
    for k in range(1, parts_ref.shape[0]):
        summed = summed + parts_ref[k].astype(F32)
    return summed


def residual_kernel(parts_ref, stream_ref, out_ref, copies_ref):
    attended = (stream_ref[...].astype(F32) + total(parts_ref)).astype(BF)
    out_ref[...] = attended
    for k in range(copies_ref.shape[0]):
        copies_ref[k] = attended


def final_kernel(parts_ref, attended_ref, out_ref):
    out_ref[...] = (attended_ref[...].astype(F32) + total(parts_ref)).astype(BF)


def widen_kernel(x_ref, gain_ref, *rest):
    weights, (out_ref, held, sems) = rest[:4], rest[4:]
    units = weights[0].shape[1]
    size = held.shape[1] // sems.shape[1]
    arriving = [
        [
            pltpu.make_async_copy(
                weights[k + 1].at[pl.ds(j * size, size)],
                held.at[k, pl.ds(j * size, size)],
                sems.at[k, j],
            )
            for j in range(sems.shape[1])
        ]
        for k in range(held.shape[0])
    ]
    for copies in arriving:
        for copy in copies:
            copy.start()
    x = x_ref[...].astype(F32)
    scaled = (x * gain_ref[...]).astype(BF)
    squares = jnp.sum(x * x, axis=1, keepdims=True)
    high = squares.astype(BF).astype(F32)
    lanes = lax.broadcasted_iota(jnp.int32, (x.shape[0], LANES), 1)
    tail = jnp.where(lanes == 0, high, jnp.where(lanes == 1, squares - high, 0.0))
    out_ref[:, 4 * units :] = tail.astype(BF)
    for k in range(4):
        if k > 0:
            for copy in arriving[k - 1]:
                copy.wait()
        weight = weights[0][...] if k == 0 else held[k - 1]
        out_ref[:, k * units : (k + 1) * units] = jnp.dot(
            scaled, weight, preferred_element_type=F32
        ).astype(BF)


def hidden_kernel(units, parts_ref, out_ref):
    sources = parts_ref.shape[0]

    def summed(start, size):
        return functools.reduce(
            lambda a, b: a + b,
            [parts_ref[k, :, start : start + size].astype(F32) for k in range(sources)],
        )

    squares = jnp.sum(summed(2 * units, LANES), axis=1, keepdims=True)
    inverse = lax.rsqrt(squares / D + EPSILON)
    for start in range(0, units, LANES):
        gate = summed(start, LANES) * inverse
        upward = summed(units + start, LANES) * inverse
        hidden = (gate / (1.0 + jnp.exp(-gate)) * upward).astype(BF)
        for k in range(out_ref.shape[0]):
            out_ref[k, :, start : start + LANES] = hidden


def on_device(
    queries,
    tree_kv,
    cache,
    ctx_len,
    parents,
    stream,
    out_weight,
    norm_gain,
    gate_weight,
    up_weight,
    down_weight,
):
    rows = lax.axis_size("row")
    cols = lax.axis_size("col")
    plane = lax.axis_size("grp") * cols
    chips = rows // 2
    far = 5 * chips // 8
    targets = [(z + far) % chips for z in range(chips)]
    ring = [[2 * z + core for z in targets] for core in range(2)]
    sources = [(p + 12) % plane for p in range(plane)]
    swap = [(r, r ^ 1) for r in range(rows)]
    nodes = queries.shape[1]
    group = queries.shape[2] // HD
    span = cache.shape[2]
    local = out_weight.shape[1]
    units = gate_weight.shape[1]
    odd = (lax.axis_index("row") % 2).astype(jnp.int32).reshape(1)

    def swapped(x):
        return lax.ppermute(x, "row", swap)

    def along_ring(x):
        return lax.all_to_all(x, "row", 0, 0, axis_index_groups=ring, tiled=True)

    def in_plane(x):
        return lax.all_to_all(x, PLANE, 0, 0, axis_index_groups=[sources], tiled=True)

    other_weight = swapped(out_weight)
    other_gate = swapped(gate_weight)
    other_up = swapped(up_weight)
    other_down = swapped(down_weight)

    width = group * HD
    pieces = 1
    lines = call(
        functools.partial(attend_kernel, nodes, group, pieces),
        shape(plane, nodes, width + LANES),
        [ANY] * 5,
        4 * nodes * group * span * HD,
        cache.size * 2,
        scratch_shapes=[
            pltpu.SMEM((1, 1), jnp.int32),
            pltpu.SMEM(parents.shape, jnp.int32),
            pltpu.VMEM(queries.shape, BF),
            pltpu.VMEM(tree_kv.shape, BF),
            pltpu.VMEM(cache.shape[1:], BF),
            pltpu.SemaphoreType.DMA((4,)),
            pltpu.SemaphoreType.DMA((2, pieces)),
        ],
        vmem=56,
    )(ctx_len.reshape(1, 1), parents, queries, tree_kv, cache)
    lines, other_weight = lax.optimization_barrier((in_plane(lines), other_weight))
    blocks = call(
        functools.partial(join_kernel, cols, group, sources, targets),
        shape(chips, nodes, D // chips),
        [SMEM, VMEM],
        4 * lines.size,
        lines.size * 2,
    )(odd, lines)
    tokens = chips * nodes
    portion = along_ring(blocks).reshape(tokens, D // chips)
    partial = call(
        project_kernel,
        shape(tokens, local),
        [VMEM, VMEM, VMEM],
        2 * tokens * local * (D // chips),
        out_weight.size * 4,
    )(portion, out_weight, other_weight)
    parts, other_gate, other_up = lax.optimization_barrier(
        (along_ring(partial.reshape(chips, nodes, local)), other_gate, other_up)
    )
    attended, copies = call(
        residual_kernel,
        (shape(nodes, local), shape(chips, nodes, local)),
        [VMEM, VMEM],
        parts.size,
        parts.size * 4,
    )(parts, stream)

    mine, other_down = lax.optimization_barrier((along_ring(copies), other_down))
    mine = mine.reshape(tokens, local)
    wide = 4 * units + LANES
    expanded = call(
        widen_kernel,
        shape(tokens, wide),
        [VMEM] * 3 + [HBM] * 3,
        8 * tokens * local * units,
        gate_weight.size * 8,
        scratch_shapes=[
            pltpu.VMEM((3,) + up_weight.shape, BF),
            pltpu.SemaphoreType.DMA((3, 1)),
        ],
    )(mine, norm_gain.reshape(1, local), gate_weight, other_gate, up_weight, other_up)
    share = tokens // plane
    gathered = in_plane(expanded.reshape(plane, share, wide))
    hidden = call(
        functools.partial(hidden_kernel, 2 * units),
        shape(plane, share, 2 * units),
        [VMEM],
        gathered.size,
        gathered.size * 2,
    )(gathered)
    hidden = in_plane(hidden).reshape(tokens, 2 * units)
    lowered = call(
        project_kernel,
        shape(tokens, local),
        [VMEM, VMEM, VMEM],
        4 * tokens * local * units,
        down_weight.size * 4,
    )(hidden, down_weight, other_down)
    parts = along_ring(lowered.reshape(chips, nodes, local))
    layer_output = call(
        final_kernel, shape(nodes, local), [VMEM, VMEM], parts.size, parts.size * 2
    )(parts, attended)
    return (attended, layer_output)


def solution(mesh):
    placed = (
        P("row", None, "col"),
        P("row", None, None, "col"),
        P("row", None, "grp", "col"),
        P("row"),
        P("row", None),
        P("row", ("grp", "col")),
        P("row", ("grp", "col")),
        P(("grp", "col")),
        P(("grp", "col"), "row"),
        P(("grp", "col"), "row"),
        P("row", ("grp", "col")),
    )
    return jax.shard_map(
        on_device,
        mesh=mesh,
        in_specs=placed,
        out_specs=(P("row", ("grp", "col")), P("row", ("grp", "col"))),
        check_vma=False,
    )
```

```python
import functools
import math

import jax
import jax.numpy as jnp
from jax import lax
from jax.experimental import pallas as pl
from jax.experimental.pallas import tpu as pltpu
from jax.sharding import PartitionSpec as P

D = 8192
HD = 128
FLOOR = -1e30
EPSILON = 1e-05
PLANE = ("grp", "col")
LANES = 128
VMEM = pl.BlockSpec(memory_space=pltpu.VMEM)
SMEM = pl.BlockSpec(memory_space=pltpu.SMEM)
ANY = pl.BlockSpec(memory_space=pl.ANY)
HBM = pl.BlockSpec(memory_space=pltpu.HBM)
BF = jnp.bfloat16
F32 = jnp.float32


def call(kernel, out_shape, in_specs, flops, moved, **more):
    return pl.pallas_call(
        kernel,
        out_shape=out_shape,
        in_specs=in_specs,
        out_specs=more.pop("out_specs", jax.tree.map(lambda unused: VMEM, out_shape)),
        cost_estimate=pl.CostEstimate(flops=flops, bytes_accessed=moved, transcendentals=0),
        compiler_params=pltpu.CompilerParams(vmem_limit_bytes=more.pop("vmem", 16) * 1024 * 1024),
        **more,
    )


def shape(*dims, kind=BF):
    return jax.ShapeDtypeStruct(dims, kind)


def attend_kernel(
    nodes,
    group,
    pieces,
    length_ref,
    parents_ref,
    q_ref,
    tree_ref,
    cache_ref,
    out_ref,
    length,
    parents,
    q_wide,
    tree_pair,
    cached,
    sems,
    cache_sems,
):
    span = cache_ref.shape[2]
    rows = nodes * group
    scale = 1.0 / math.sqrt(HD)
    small = [
        pltpu.make_async_copy(source, target, sems.at[k])
        for k, (source, target) in enumerate(
            [(q_ref, q_wide), (length_ref, length), (parents_ref, parents), (tree_ref, tree_pair)]
        )
    ]
    size = span // pieces
    large = [
        pltpu.make_async_copy(
            cache_ref.at[0, part, pl.ds(k * size, size)],
            cached.at[part, pl.ds(k * size, size)],
            cache_sems.at[part, k],
        )
        for part in range(2)
        for k in range(pieces)
    ]
    for copy in large[:pieces] + small + large[pieces:]:
        copy.start()
    for copy in small:
        copy.wait()
    place = lax.axis_index("grp")
    limit = length[0, 0] - place * span
    tree_here = (place == lax.axis_size("grp") - 1).astype(jnp.int32)

    wide = q_wide[0].astype(F32)
    q = jnp.concatenate([wide[:, h * HD : (h + 1) * HD] for h in range(group)], axis=0).astype(BF)
    contract = (((1,), (1,)), ((), ()))

    lane = lax.broadcasted_iota(jnp.int32, (nodes, nodes), 1)
    here = lax.broadcasted_iota(jnp.int32, (nodes, nodes), 0)
    reach = jnp.zeros((nodes, nodes), jnp.int32)
    for unused in range(nodes):
        reach = jnp.where(lane == here, 1, reach)
        above = jnp.full((nodes, nodes), -1, jnp.int32)
        for j in range(nodes):
            above = jnp.where(here == j, parents[0, j], above)
        here = above
    reach = jnp.concatenate([reach * tree_here] * group, axis=0)
    pair = tree_pair[0].astype(F32)
    tree_keys = pair[:, 0, :].astype(BF)
    tree_values = pair[:, 1, :]
    tree_scores = lax.dot_general(q, tree_keys, contract, preferred_element_type=F32) * scale
    tree_scores = jnp.where(reach > 0, tree_scores, FLOOR)
    maxima = jnp.max(tree_scores, axis=1, keepdims=True)

    for copy in large[:pieces]:
        copy.wait()
    scores = lax.dot_general(q, cached[0], contract, preferred_element_type=F32) * scale
    position = lax.broadcasted_iota(jnp.int32, (rows, span), 1)
    scores = jnp.where(position < limit, scores, FLOOR)
    maxima = jnp.maximum(maxima, jnp.max(scores, axis=1, keepdims=True))
    tree_weights = jnp.exp(tree_scores - maxima)
    totals = jnp.sum(tree_weights, axis=1, keepdims=True)
    tree_rounded = tree_weights.astype(BF).astype(F32)
    summed = jnp.zeros((rows, HD), F32)
    for j in range(nodes):
        summed = summed + tree_rounded[:, j : j + 1] * tree_values[j : j + 1, :]
    weights = jnp.exp(scores - maxima)
    totals = totals + jnp.sum(weights, axis=1, keepdims=True)
    for copy in large[pieces:]:
        copy.wait()
    summed = summed + jnp.dot(weights.astype(BF), cached[1], preferred_element_type=F32)
    heads = summed / totals
    level = maxima + jnp.log(totals)

    high = level.astype(BF).astype(F32)
    middle = (level - high).astype(BF).astype(F32)
    low = level - high - middle
    lanes = lax.broadcasted_iota(jnp.int32, (nodes, LANES), 1)
    tail = jnp.zeros((nodes, LANES), F32)
    for h in range(group):
        for k, part in enumerate((high, middle, low)):
            tail = jnp.where(lanes == k * group + h, part[h * nodes : (h + 1) * nodes], tail)
    line = jnp.concatenate(
        [heads[h * nodes : (h + 1) * nodes] for h in range(group)] + [tail], axis=1
    ).astype(BF)
    for k in range(out_ref.shape[0]):
        out_ref[k] = line


def join_kernel(cols, group, sources, targets, odd_ref, in_ref, out_ref):
    width = group * HD
    odd = odd_ref[0] > 0
    per_block = out_ref.shape[2] // HD
    block = []
    for c in range(cols):
        levels = []
        for g in range(2):
            tail = in_ref[sources.index(g * cols + c), :, width:].astype(F32)
            levels.append(
                tail + jnp.roll(tail, -group, axis=1) + jnp.roll(tail, -2 * group, axis=1)
            )
        share = 1.0 / (1.0 + jnp.exp(levels[1] - levels[0]))
        for h in range(group):
            near = in_ref[sources.index(c), :, h * HD : (h + 1) * HD].astype(F32)
            far = in_ref[sources.index(cols + c), :, h * HD : (h + 1) * HD].astype(F32)
            block.append(far + (near - far) * share[:, h : h + 1])
            if len(block) == per_block:
                half = per_block // 2
                first = jnp.concatenate(block[:half], axis=1)
                second = jnp.concatenate(block[half:], axis=1)
                mine = jnp.where(odd, second, first)
                other = jnp.where(odd, first, second)
                number = (c * group + h) // per_block
                out_ref[targets.index(number)] = jnp.concatenate([mine, other], axis=1).astype(BF)
                block = []


def project_kernel(a_ref, mine_ref, other_ref, out_ref):
    half = mine_ref.shape[0]
    out_ref[...] = (
        jnp.dot(a_ref[:, :half], mine_ref[...], preferred_element_type=F32)
        + jnp.dot(a_ref[:, half:], other_ref[...], preferred_element_type=F32)
    ).astype(BF)


def total(parts_ref):
    summed = parts_ref[0].astype(F32)
    for k in range(1, parts_ref.shape[0]):
        summed = summed + parts_ref[k].astype(F32)
    return summed


def residual_kernel(parts_ref, stream_ref, out_ref, copies_ref):
    attended = (stream_ref[...].astype(F32) + total(parts_ref)).astype(BF)
    out_ref[...] = attended
    for k in range(copies_ref.shape[0]):
        copies_ref[k] = attended


def final_kernel(parts_ref, attended_ref, out_ref):
    out_ref[...] = (attended_ref[...].astype(F32) + total(parts_ref)).astype(BF)


def widen_kernel(x_ref, gain_ref, *rest):
    weights, (out_ref, held, sems) = rest[:4], rest[4:]
    units = weights[0].shape[1]
    size = held.shape[1] // sems.shape[1]
    arriving = [
        [
            pltpu.make_async_copy(
                weights[k + 1].at[pl.ds(j * size, size)],
                held.at[k, pl.ds(j * size, size)],
                sems.at[k, j],
            )
            for j in range(sems.shape[1])
        ]
        for k in range(held.shape[0])
    ]
    for copies in arriving:
        for copy in copies:
            copy.start()
    x = x_ref[...].astype(F32)
    scaled = (x * gain_ref[...]).astype(BF)
    squares = jnp.sum(x * x, axis=1, keepdims=True)
    high = squares.astype(BF).astype(F32)
    lanes = lax.broadcasted_iota(jnp.int32, (x.shape[0], LANES), 1)
    tail = jnp.where(lanes == 0, high, jnp.where(lanes == 1, squares - high, 0.0))
    out_ref[:, 4 * units :] = tail.astype(BF)
    for k in range(4):
        if k > 0:
            for copy in arriving[k - 1]:
                copy.wait()
        weight = weights[0][...] if k == 0 else held[k - 1]
        out_ref[:, k * units : (k + 1) * units] = jnp.dot(
            scaled, weight, preferred_element_type=F32
        ).astype(BF)


def hidden_kernel(units, parts_ref, out_ref):
    sources = parts_ref.shape[0]

    def summed(start, size):
        return functools.reduce(
            lambda a, b: a + b,
            [parts_ref[k, :, start : start + size].astype(F32) for k in range(sources)],
        )

    squares = jnp.sum(summed(2 * units, LANES), axis=1, keepdims=True)
    inverse = lax.rsqrt(squares / D + EPSILON)
    for start in range(0, units, LANES):
        gate = summed(start, LANES) * inverse
        upward = summed(units + start, LANES) * inverse
        hidden = (gate / (1.0 + jnp.exp(-gate)) * upward).astype(BF)
        for k in range(out_ref.shape[0]):
            out_ref[k, :, start : start + LANES] = hidden


def on_device(
    queries,
    tree_kv,
    cache,
    ctx_len,
    parents,
    stream,
    out_weight,
    norm_gain,
    gate_weight,
    up_weight,
    down_weight,
):
    rows = lax.axis_size("row")
    cols = lax.axis_size("col")
    plane = lax.axis_size("grp") * cols
    chips = rows // 2
    far = 5 * chips // 8
    targets = [(z + far) % chips for z in range(chips)]
    ring = [[2 * z + core for z in targets] for core in range(2)]
    sources = [(p + 12) % plane for p in range(plane)]
    swap = [(r, r ^ 1) for r in range(rows)]
    nodes = queries.shape[1]
    group = queries.shape[2] // HD
    span = cache.shape[2]
    local = out_weight.shape[1]
    units = gate_weight.shape[1]
    odd = (lax.axis_index("row") % 2).astype(jnp.int32).reshape(1)

    def swapped(x):
        return lax.ppermute(x, "row", swap)

    def along_ring(x):
        return lax.all_to_all(x, "row", 0, 0, axis_index_groups=ring, tiled=True)

    def in_plane(x):
        return lax.all_to_all(x, PLANE, 0, 0, axis_index_groups=[sources], tiled=True)

    other_weight = swapped(out_weight)
    other_gate = swapped(gate_weight)
    other_up = swapped(up_weight)
    other_down = swapped(down_weight)

    width = group * HD
    pieces = 1
    lines = call(
        functools.partial(attend_kernel, nodes, group, pieces),
        shape(plane, nodes, width + LANES),
        [ANY] * 5,
        4 * nodes * group * span * HD,
        cache.size * 2,
        scratch_shapes=[
            pltpu.SMEM((1, 1), jnp.int32),
            pltpu.SMEM(parents.shape, jnp.int32),
            pltpu.VMEM(queries.shape, BF),
            pltpu.VMEM(tree_kv.shape, BF),
            pltpu.VMEM(cache.shape[1:], BF),
            pltpu.SemaphoreType.DMA((4,)),
            pltpu.SemaphoreType.DMA((2, pieces)),
        ],
        vmem=56,
    )(ctx_len.reshape(1, 1), parents, queries, tree_kv, cache)
    lines, other_weight = lax.optimization_barrier((in_plane(lines), other_weight))
    blocks = call(
        functools.partial(join_kernel, cols, group, sources, targets),
        shape(chips, nodes, D // chips),
        [SMEM, VMEM],
        4 * lines.size,
        lines.size * 2,
    )(odd, lines)
    tokens = chips * nodes
    portion = along_ring(blocks).reshape(tokens, D // chips)
    partial = call(
        project_kernel,
        shape(tokens, local),
        [VMEM, VMEM, VMEM],
        2 * tokens * local * (D // chips),
        out_weight.size * 4,
    )(portion, out_weight, other_weight)
    parts, other_gate, other_up = lax.optimization_barrier(
        (along_ring(partial.reshape(chips, nodes, local)), other_gate, other_up)
    )
    attended, copies = call(
        residual_kernel,
        (shape(nodes, local), shape(chips, nodes, local)),
        [VMEM, VMEM],
        parts.size,
        parts.size * 4,
    )(parts, stream)

    mine, other_down = lax.optimization_barrier((along_ring(copies), other_down))
    mine = mine.reshape(tokens, local)
    wide = 4 * units + LANES
    expanded = call(
        widen_kernel,
        shape(tokens, wide),
        [VMEM] * 3 + [HBM] * 3,
        8 * tokens * local * units,
        gate_weight.size * 8,
        scratch_shapes=[
            pltpu.VMEM((3,) + up_weight.shape, BF),
            pltpu.SemaphoreType.DMA((3, 2)),
        ],
    )(mine, norm_gain.reshape(1, local), gate_weight, other_gate, up_weight, other_up)
    share = tokens // plane
    gathered = in_plane(expanded.reshape(plane, share, wide))
    hidden = call(
        functools.partial(hidden_kernel, 2 * units),
        shape(plane, share, 2 * units),
        [VMEM],
        gathered.size,
        gathered.size * 2,
    )(gathered)
    hidden = in_plane(hidden).reshape(tokens, 2 * units)
    lowered = call(
        project_kernel,
        shape(tokens, local),
        [VMEM, VMEM, VMEM],
        4 * tokens * local * units,
        down_weight.size * 4,
    )(hidden, down_weight, other_down)
    parts = along_ring(lowered.reshape(chips, nodes, local))
    layer_output = call(
        final_kernel, shape(nodes, local), [VMEM, VMEM], parts.size, parts.size * 2
    )(parts, attended)
    return (attended, layer_output)


def solution(mesh):
    placed = (
        P("row", None, "col"),
        P("row", None, None, "col"),
        P("row", None, "grp", "col"),
        P("row"),
        P("row", None),
        P("row", ("grp", "col")),
        P("row", ("grp", "col")),
        P(("grp", "col")),
        P(("grp", "col"), "row"),
        P(("grp", "col"), "row"),
        P("row", ("grp", "col")),
    )
    return jax.shard_map(
        on_device,
        mesh=mesh,
        in_specs=placed,
        out_specs=(P("row", ("grp", "col")), P("row", ("grp", "col"))),
        check_vma=False,
    )
```
